32 devices in a mesh: tm: 16 (over z, y, x), state: 2 (over core).
Axes of the slice: x: 2, y: 2, z: 4, core: 2. Of those that a mesh axis runs over, the one named last changes fastest.
Arguments:
- features: float32 [4, 256, 512], P(None, 'tm'), may hold values from -18 to 18
- gauss_means: float32 [1024, 512], P('state'), may hold values from -3 to 3
- precisions: float32 [1024, 512], P('state'), may hold values from 0.5 to 2
- transitions: bfloat16 [1024, 1024], P('state'), may hold values from 0 to 1, as said below
- initial: bfloat16 [1024], P('state'), may hold values from 0.099609375 to 10
- reset_flags: int32 [4, 256], P(None, 'tm'), may hold values from 0 to 1, as said below
Outputs:
- posteriors: bfloat16 [4, 256, 1024], P(None, 'tm', 'state')
- evidence: float32 [4, 256], P(None, ('tm', 'state'))
The draws below stay inside these ranges and needn't reach their ends.
Inputs may be any that keep to these rules, and one draw needn't show every extreme that they name: `transitions`: every entry nonnegative; each row sums to 1 up to the rounding of its entries; the diagonal holds half or more of each row. reset_flags[b, 0] = 1 in every stream; the runs of frames from one 1 to the next (utterances) hold 1 to 16 frames, and some hold exactly 16.
All inputs are finite; a program needn't handle non-finite values.
Results may differ from the reference program's by a relative error of at most 0.012.
Values may be sent and summed in bfloat16 or wider, within the bound.
A program may use at most 64 MiB of HBM per device.

```python
import math
import jax
import jax.numpy as jnp
from jax import lax

S = 1024
F = 512
STREAMS = 4
MAXLEN = 16
FRAMES = 256


def draw_features(key, part):
    noise = jnp.clip(jax.random.normal(jax.random.fold_in(key, 11), (STREAMS, FRAMES, F), jnp.float32), -6.0, 6.0)
    frame_scale = jnp.exp(jax.random.uniform(jax.random.fold_in(key, 12), (STREAMS, FRAMES, 1), jnp.float32, jnp.log(0.5), jnp.log(3.0)))
    return noise * frame_scale


def draw_transitions(key, part):
    staying = jax.random.uniform(jax.random.fold_in(key, 21), (S,), jnp.float32, 0.5, 0.9)
    leaving = jnp.exp(jax.random.uniform(jax.random.fold_in(key, 22), (S, S), jnp.float32, jnp.log(0.1), jnp.log(10.0)))
    leaving = leaving * (1.0 - jnp.eye(S, dtype=jnp.float32))
    leaving = leaving / jnp.sum(leaving, axis=1, keepdims=True) * (1.0 - staying)[:, None]
    return (leaving + jnp.diag(staying)).astype(jnp.bfloat16)


def draw_reset_flags(key, part):
    shortest = max(MAXLEN // 2, 1)
    count = FRAMES // shortest + 2
    lengths = jax.random.randint(jax.random.fold_in(key, 31), (STREAMS, count), shortest, MAXLEN + 1)
    lengths = lengths.at[:, 0].set(MAXLEN - 1)
    lengths = lengths.at[:, 1].set(MAXLEN)
    starts = jnp.cumsum(lengths, axis=1) - lengths

    def marked(row_starts):
        return jnp.zeros((FRAMES,), jnp.int32).at[row_starts].set(1, mode='drop')
    return jax.vmap(marked)(starts)


def block_scale(rng, shape, pieces, low, high):
    def one(axis_at, shards_of):
        draws = jax.random.uniform(jax.random.fold_in(jax.random.fold_in(rng, 6), axis_at), (shards_of,), jnp.float32, low / len(pieces), high / len(pieces))
        return jnp.repeat(jnp.exp(draws), shape[axis_at] // shards_of).reshape((-1,) + (1,) * (len(shape) - axis_at - 1))

    level = one(*pieces[0])
    for cut in pieces[1:]:
        level = level * one(*cut)
    return level


def scatter_about(rng, dims, scale, reach, cuts=(), kind=jnp.bfloat16):
    gain = block_scale(rng, dims, cuts, -0.22, 0.18) if cuts else 1.0
    values = jax.random.normal(rng, dims, jnp.float32) * scale * gain
    return jnp.minimum(jnp.maximum(values, -reach), reach).astype(kind)


def setup_inputs(seed: int = 0) -> dict:
    streams_of = jax.random.split(jax.random.key(seed), 7)
    features = draw_features(jax.random.fold_in(streams_of[6], 71), 0)
    gauss_means = scatter_about(streams_of[1], (S, F), 0.5, 3.0, ((0, 2),), jnp.float32)
    precisions = jnp.clip(jnp.exp(math.log(2.0) - 1.3862944 * jax.random.uniform(streams_of[2], (S, F), jnp.float32) ** block_scale(streams_of[2], (S, F), ((0, 2),), -0.2, 0.2)), 0.5, 2.0)
    transitions = draw_transitions(jax.random.fold_in(streams_of[6], 71), 0)
    initial = jnp.clip(jnp.exp(math.log(10.0) - 4.609084 * jax.random.uniform(streams_of[4], (S,), jnp.float32) ** block_scale(streams_of[4], (S,), ((0, 2),), -0.2, 0.2)), 0.099609375, 10.0).astype(jnp.bfloat16)
    reset_flags = draw_reset_flags(jax.random.fold_in(streams_of[6], 71), 0)
    return dict(features=features, gauss_means=gauss_means, precisions=precisions, transitions=transitions, initial=initial, reset_flags=reset_flags)


acoustic = 0.1


def reference(features, gauss_means, precisions, transitions, initial, reset_flags):
    streams, frames, feat_width = features.shape
    states = gauss_means.shape[0]
    highest = lax.Precision.HIGHEST
    flat_feats = features.reshape(streams * frames, feat_width)
    quadratic = jnp.dot(flat_feats * flat_feats, (-0.5 * precisions).T, precision=highest)
    linear_part = jnp.dot(flat_feats, (precisions * gauss_means).T, precision=highest)
    offset = 0.5 * jnp.sum(jnp.log(precisions) - precisions * gauss_means * gauss_means, axis=1)
    scores = (acoustic * (quadratic + linear_part + offset)).reshape(streams, frames, states)
    maxima = jnp.max(scores, axis=2, keepdims=True)
    emission_t = jnp.swapaxes(jnp.exp(scores - maxima), 0, 1)
    reset_t = jnp.swapaxes(reset_flags, 0, 1)
    prior_float = initial.astype(jnp.float32)
    prior_dist = prior_float / jnp.sum(prior_float)
    trans_back = transitions.T

    def forward_step(alpha_prev, inputs):
        emit_row, reset_row = inputs
        predicted = jnp.dot(alpha_prev.astype(jnp.bfloat16), transitions, preferred_element_type=jnp.float32)
        predicted = jnp.where(reset_row[:, None] == 1, prior_dist[None, :], predicted)
        weighted = emit_row * predicted
        norm_total = jnp.sum(weighted, axis=1)
        alpha_next = weighted / norm_total[:, None]
        return alpha_next, (alpha_next, jnp.log(norm_total))

    alpha_start = jnp.zeros((streams, states), jnp.float32)
    alpha_last, (alphas, log_norms) = lax.scan(forward_step, alpha_start, (emission_t, reset_t))

    def backward_step(beta_next, inputs):
        emit_row, reset_row = inputs
        spread = jnp.dot((emit_row * beta_next).astype(jnp.bfloat16), trans_back, preferred_element_type=jnp.float32)
        spread = spread / jnp.sum(spread, axis=1, keepdims=True)
        beta_prev = jnp.where(reset_row[:, None] == 1, 1.0 / states, spread)
        return beta_prev, beta_next

    beta_start = jnp.full((streams, states), 1.0 / states, jnp.float32)
    beta_first, betas = lax.scan(backward_step, beta_start, (emission_t, reset_t), reverse=True)
    product = alphas * betas
    posterior = (product / jnp.sum(product, axis=2, keepdims=True)).astype(jnp.bfloat16)
    return jnp.swapaxes(posterior, 0, 1), jnp.swapaxes(log_norms, 0, 1)
```

```python
import functools

import jax
import jax.numpy as jnp
from jax import lax
from jax.experimental import pallas as pl
from jax.experimental.pallas import tpu as pltpu
from jax.sharding import PartitionSpec as P

MAXLEN = 16
ACOUSTIC = 0.1
MESH = pl.DeviceIdType.MESH
F32 = jnp.float32
BF16 = jnp.bfloat16
PAD = 8
LANES = 128


def split(a):
    hi = a.astype(BF16)
    return hi, (a - hi.astype(F32)).astype(BF16)


def dot_t(a, b):
    return lax.dot_general(a, b, (((1,), (1,)), ((), ())), preferred_element_type=F32)


def kernel(
    blocks, feat, means, prec, trans, init, flags, post, evid,
    xin, raw, wt, prior_in, w_hi, w_lo, sc, sc_in, em, xb, y, inv, flag_pad, mask, fin, fin_in,
    send, recv,
):
    c = lax.axis_index("tm")
    s = lax.axis_index("state")
    o = 1 - s
    nxt = lax.rem(c + 1, blocks)
    prv = lax.rem(c + blocks - 1, blocks)
    streams, frames, width = feat.shape
    half = trans.shape[0]
    states = trans.shape[1]
    rows = streams * frames
    chunk = min(256, states)

    barrier = pltpu.get_barrier_semaphore()
    for who in ((nxt, s), (prv, s), (c, o)):
        pl.semaphore_signal(barrier, inc=1, device_id=who, device_id_type=MESH)

    row_t = lax.broadcasted_iota(jnp.int32, (frames, frames), 0)
    col_t = lax.broadcasted_iota(jnp.int32, (frames, frames), 1)
    for b in range(streams):
        at = rows + b * frames
        xin[at : at + frames, :width] = feat[b]
        line = jnp.broadcast_to(flags[b : b + 1, :].astype(F32), (frames, frames))
        column = jnp.sum(jnp.where(row_t == col_t, line, 0.0), axis=1, keepdims=True)
        xin[at : at + frames, width:] = jnp.broadcast_to(column, (frames, LANES))
    mine = pl.ds(pl.multiple_of(s * half, half), half)
    theirs = pl.ds(pl.multiple_of(o * half, half), half)
    prior_in[:, mine] = jnp.broadcast_to(init[...].astype(F32), (8, half))

    pl.semaphore_wait(barrier, 3)

    def remote(src, dst, k, who):
        return pltpu.make_async_remote_copy(
            src_ref=src, dst_ref=dst, send_sem=send.at[k], recv_sem=recv.at[k],
            device_id=who, device_id_type=MESH,
        )

    own = xin.at[pl.ds(rows, rows)]
    to_next = remote(own, xin.at[pl.ds(0, rows)], 0, (nxt, s))
    to_prev = remote(own, xin.at[pl.ds(2 * rows, rows)], 1, (prv, s))
    trans_copy = remote(trans, raw.at[mine], 2, (c, o))
    prior_copy = remote(prior_in.at[:, mine], prior_in.at[:, mine], 3, (c, o))
    to_next.start()
    to_prev.start()
    trans_copy.start()
    prior_copy.start()

    p = prec[...]
    m = means[...]
    pm = p * m
    hi, lo = split(-0.5 * p)
    w_hi[:, :width] = hi
    w_lo[:, :width] = lo
    hi, lo = split(pm)
    w_hi[:, width:] = hi
    w_lo[:, width:] = lo
    offset = 0.5 * jnp.sum(jnp.log(p) - pm * m, axis=1, keepdims=True)
    offset = jnp.broadcast_to(offset, (half, LANES)).T[0:1]
    raw[mine, :] = trans[...]

    @pl.when(s == 1)
    def _():
        wt[:, half:] = trans[...].T

    to_next.wait_recv()
    to_prev.wait_recv()
    x = xin[:, :width]
    sq_hi, sq_lo = split(x * x)
    x_hi, x_lo = split(x)
    left_hi = jnp.concatenate([sq_hi, x_hi], axis=1)
    left_lo = jnp.concatenate([sq_lo, x_lo], axis=1)
    total = dot_t(left_hi, w_hi[...]) + (dot_t(left_lo, w_hi[...]) + dot_t(left_hi, w_lo[...]))
    sc[...] = ACOUSTIC * (total + offset)

    window = pl.ds(pl.multiple_of(s * rows, rows), 2 * rows)
    other_window = pl.ds(pl.multiple_of(o * rows, rows), 2 * rows)
    score_copy = remote(sc.at[other_window], sc_in, 4, (c, o))
    score_copy.start()

    trans_copy.wait_recv()
    prior_copy.wait_recv()

    @pl.when(s == 1)
    def _():
        wt[:, :half] = raw[:half, :].T

    flag_pad[...] = jnp.ones_like(flag_pad)
    y[:, :PAD] = jnp.ones((streams, PAD, states), F32)
    y[:, PAD + 2 * frames :] = jnp.ones((streams, PAD, states), F32)
    for h in range(2):
        for b in range(streams):
            at = pl.multiple_of((s + h) * rows + b * frames, frames)
            flag_pad[b, PAD + h * frames : PAD + (h + 1) * frames] = xin[pl.ds(at, frames), width:]

    score_copy.wait_recv()
    for i in range(0, 2 * rows, 32):
        at = pl.multiple_of(s * rows + i, 32)
        a = sc[pl.ds(at, 32)]
        z = sc_in[i : i + 32]
        top = jnp.maximum(jnp.max(a, axis=1, keepdims=True), jnp.max(z, axis=1, keepdims=True))
        em[i : i + 32, mine] = jnp.exp(a - top)
        em[i : i + 32, theirs] = jnp.exp(z - top)

    pieces = [(h, b, (h * streams + b) * frames) for h in range(2) for b in range(streams)]

    def spread(a):
        return jnp.concatenate([a] * (chunk // LANES), axis=1)

    def chain(weights, forward):
        d = -1 if forward else 1
        held = 1 if forward else 0
        if forward:
            prior = prior_in[...]
            prior = prior / jnp.sum(prior, axis=1, keepdims=True)
        else:
            prior = jnp.full((8, states), 1.0 / states, F32)
        base = prior[0:1]

        for h, b, r in pieces:
            first = PAD + h * frames + (0 if forward else 1)
            mask[r : r + frames] = flag_pad[b, first : first + frames]
            x0 = em[r : r + frames] * base
            xb[0, r : r + frames] = x0.astype(BF16)
            inv[r : r + frames] = jnp.broadcast_to(
                1.0 / jnp.sum(x0, axis=1, keepdims=True), (frames, LANES)
            )

        def step(now, later, last):
            sums = [None] * len(pieces)
            for n in range(0, states, chunk):
                cols = slice(n, n + chunk)
                out = jnp.dot(xb[now], weights[:, cols], preferred_element_type=F32)
                for h, b, r in pieces:
                    at = PAD + h * frames
                    y[b, at : at + frames, cols] = out[r : r + frames] * spread(inv[r : r + frames])
                for k, (h, b, r) in enumerate(pieces):
                    if last and h != held:
                        continue
                    at = PAD + h * frames + d
                    reset = spread(mask[r : r + frames]) > 0.5
                    value = jnp.where(reset, base[:, cols], y[b, at : at + frames, cols])
                    if last and not forward:
                        fin[b * frames : (b + 1) * frames, cols] = value
                        continue
                    value = em[r : r + frames, cols] * value
                    if last:
                        fin[b * frames : (b + 1) * frames, cols] = value
                    else:
                        xb[later, r : r + frames, cols] = value.astype(BF16)
                    part = sum(value[:, i : i + LANES] for i in range(0, chunk, LANES))
                    sums[k] = part if sums[k] is None else sums[k] + part
            for k, (h, b, r) in enumerate(pieces):
                if sums[k] is None:
                    continue
                norm = jnp.sum(sums[k], axis=1, keepdims=True)
                if last:
                    at = b * frames
                    fin[at : at + frames, :states] = fin[at : at + frames, :states] / norm
                    fin[at : at + frames, states:] = jnp.broadcast_to(jnp.log(norm), (frames, LANES))
                else:
                    inv[r : r + frames] = jnp.broadcast_to(1.0 / norm, (frames, LANES))

        def two(i, carry):
            step(0, 1, False)
            step(1, 0, False)
            return carry

        turns = MAXLEN - 2
        lax.fori_loop(0, turns // 2, two, 0)
        if turns % 2:
            step(0, 1, False)
        step(turns % 2, 1 - turns % 2, True)
        if not forward:
            fin[:, states:] = jnp.zeros((rows, LANES), F32)

    @pl.when(s == 0)
    def _():
        chain(raw, True)

    @pl.when(s == 1)
    def _():
        chain(wt, False)

    fin_copy = remote(fin, fin_in, 5, (c, o))
    fin_copy.start()
    fin_copy.wait_recv()
    for b in range(streams):
        at = b * frames
        rows_b = slice(at, at + frames)
        product = fin[rows_b, :states] * fin_in[rows_b, :states]
        scale = 1.0 / jnp.sum(product, axis=1, keepdims=True)
        post[b] = (fin[rows_b, mine] * fin_in[rows_b, mine] * scale).astype(BF16)

    part = frames // 2
    row_e = lax.broadcasted_iota(jnp.int32, (part, LANES), 0)
    col_e = lax.broadcasted_iota(jnp.int32, (part, LANES), 1)
    for b in range(streams):
        at = pl.ds(pl.multiple_of(b * frames + s * part, part), part)
        logs = fin[at, states:] + fin_in[at, states:]
        line = jnp.sum(jnp.where(row_e == col_e, logs, 0.0), axis=0, keepdims=True)
        evid[b : b + 1, :] = line[:, :part]

    for copy in (to_next, to_prev, trans_copy, prior_copy, score_copy, fin_copy):
        copy.wait_send()


def per_device(features, gauss_means, precisions, transitions, initial, reset_flags):
    streams, frames, width = features.shape
    half, states = transitions.shape
    rows = streams * frames
    blocks = lax.axis_size("tm")
    vmem = pl.BlockSpec(memory_space=pltpu.VMEM)
    return pl.pallas_call(
        functools.partial(kernel, blocks),
        out_shape=(
            jax.ShapeDtypeStruct((streams, frames, half), BF16),
            jax.ShapeDtypeStruct((streams, frames // 2), F32),
        ),
        in_specs=[vmem] * 6,
        out_specs=(vmem, vmem),
        scratch_shapes=[
            pltpu.VMEM((3 * rows, width + LANES), F32),
            pltpu.VMEM((states, states), BF16),
            pltpu.VMEM((states, states), BF16),
            pltpu.VMEM((8, states), F32),
            pltpu.VMEM((half, 2 * width), BF16),
            pltpu.VMEM((half, 2 * width), BF16),
            pltpu.VMEM((3 * rows, half), F32),
            pltpu.VMEM((2 * rows, half), F32),
            pltpu.VMEM((2 * rows, states), F32),
            pltpu.VMEM((2, 2 * rows, states), BF16),
            pltpu.VMEM((streams, 2 * frames + 2 * PAD, states), F32),
            pltpu.VMEM((2 * rows, LANES), F32),
            pltpu.VMEM((streams, 2 * frames + 2 * PAD, LANES), F32),
            pltpu.VMEM((2 * rows, LANES), F32),
            pltpu.VMEM((rows, states + LANES), F32),
            pltpu.VMEM((rows, states + LANES), F32),
            pltpu.SemaphoreType.DMA((6,)),
            pltpu.SemaphoreType.DMA((6,)),
        ],
        compiler_params=pltpu.CompilerParams(
            collective_id=0, has_side_effects=True, vmem_limit_bytes=40 * 1024 * 1024
        ),
    )(features, gauss_means, precisions, transitions, initial.reshape(1, half), reset_flags)


def solution(mesh):
    return jax.shard_map(
        per_device,
        mesh=mesh,
        in_specs=(
            P(None, "tm", None),
            P("state", None),
            P("state", None),
            P("state", None),
            P("state"),
            P(None, "tm"),
        ),
        out_specs=(P(None, "tm", "state"), P(None, ("tm", "state"))),
        check_vma=False,
    )
```

```python
import functools

import jax
import jax.numpy as jnp
from jax import lax
from jax.experimental import pallas as pl
from jax.experimental.pallas import tpu as pltpu
from jax.sharding import PartitionSpec as P

MAXLEN = 16
ACOUSTIC = 0.1
MESH = pl.DeviceIdType.MESH
F32 = jnp.float32
BF16 = jnp.bfloat16
PAD = 8
LANES = 128


def split(a):
    hi = a.astype(BF16)
    return hi, (a - hi.astype(F32)).astype(BF16)


def dot_t(a, b):
    return lax.dot_general(a, b, (((1,), (1,)), ((), ())), preferred_element_type=F32)


def kernel(
    blocks, feat, means_hbm, prec_hbm, trans, init_hbm, flags_hbm, post, evid,
    means, prec, init, flags, xin, flag_in, raw, wt, lines, w_hi, w_lo, sc, halo, em, xb, y, inv, flag_pad, mask, fin, fin_in,
    send, recv, load,
):
    c = lax.axis_index("tm")
    s = lax.axis_index("state")
    o = 1 - s
    target = c + 1 - 2 * s
    source = c - 1 + 2 * s
    has_target = jnp.logical_and(target >= 0, target < blocks)
    has_source = jnp.logical_and(source >= 0, source < blocks)
    has_next = c + 1 < blocks
    has_prev = c > 0

    streams, frames, width = feat.shape
    half = trans.shape[0]
    states = trans.shape[1]
    rows = streams * frames
    chunk = min(256, states)

    barrier = pltpu.get_barrier_semaphore()

    @pl.when(has_source)
    def _():
        for core in range(2):
            pl.semaphore_signal(barrier, inc=1, device_id=(source, core), device_id_type=MESH)

    pl.semaphore_signal(barrier, inc=1, device_id=(c, o), device_id_type=MESH)

    mine = pl.ds(pl.multiple_of(s * half, half), half)
    theirs = pl.ds(pl.multiple_of(o * half, half), half)

    loads = [
        pltpu.make_async_copy(src, dst, load.at[k])
        for k, (src, dst) in enumerate(
            (
                (flags_hbm, flags),
                (init_hbm, init),
                (prec_hbm, prec),
                (means_hbm, means),
                (trans, raw.at[mine]),
                (feat, xin),
            )
        )
    ]
    for copy in loads:
        copy.start()

    row_t = lax.broadcasted_iota(jnp.int32, (frames, frames), 0)
    col_t = lax.broadcasted_iota(jnp.int32, (frames, frames), 1)
    loads[0].wait()
    for b in range(streams):
        line = jnp.broadcast_to(flags[b : b + 1, :].astype(F32), (frames, frames))
        column = jnp.sum(jnp.where(row_t == col_t, line, 0.0), axis=1, keepdims=True)
        flag_in[o, b] = jnp.broadcast_to(column, (frames, LANES))
    loads[1].wait()
    lines[:, mine] = jnp.broadcast_to(init[...].astype(F32).reshape(1, half), (8, half))

    def remote(src, dst, k, who):
        return pltpu.make_async_remote_copy(
            src_ref=src, dst_ref=dst, send_sem=send.at[k], recv_sem=recv.at[k],
            device_id=who, device_id_type=MESH,
        )

    flag_copy = remote(flag_in.at[o], flag_in.at[s], 1, (target, s))
    trans_copy = remote(trans, raw.at[mine], 2, (c, o))
    line_copy = remote(lines.at[:, mine], lines.at[:, mine], 3, (c, o))
    score_copy = remote(sc.at[s], sc.at[s], 4, (c, o))
    next_copy = remote(sc.at[s], halo.at[s], 6 + s, (c + 1, 0))
    prev_copy = pltpu.make_async_remote_copy(
        src_ref=sc.at[s], dst_ref=halo.at[s], send_sem=send.at[0], recv_sem=recv.at[6 + s],
        device_id=(c - 1, 1), device_id_type=MESH,
    )

    loads[2].wait()
    loads[3].wait()
    p = prec[...]
    m = means[...]
    pm = p * m
    hi, lo = split(-0.5 * p)
    w_hi[:, :width] = hi
    w_lo[:, :width] = lo
    hi, lo = split(pm)
    w_hi[:, width:] = hi
    w_lo[:, width:] = lo
    offset = 0.5 * jnp.sum(jnp.log(p) - pm * m, axis=1, keepdims=True)
    offset = jnp.broadcast_to(offset, (half, LANES)).T[0:1]
    loads[5].wait()
    x = xin[...].reshape(rows, width)
    sq_hi, sq_lo = split(x * x)
    x_hi, x_lo = split(x)
    left_hi = jnp.concatenate([sq_hi, x_hi], axis=1)
    left_lo = jnp.concatenate([sq_lo, x_lo], axis=1)
    both = dot_t(jnp.concatenate([left_hi, left_lo], axis=0), w_hi[...])
    total = both[:rows] + (both[rows:] + dot_t(left_hi, w_lo[...]))
    sc[s] = ACOUSTIC * (total + offset)

    pl.semaphore_wait(barrier, 1 + has_next.astype(jnp.int32) + has_prev.astype(jnp.int32))

    @pl.when(has_next)
    def _():
        next_copy.start()

    @pl.when(has_prev)
    def _():
        prev_copy.start()

    @pl.when(has_target)
    def _():
        flag_copy.start()

    score_copy.start()
    line_copy.start()
    trans_copy.start()
    loads[4].wait()

    @pl.when(s == 1)
    def _():
        wt[:, half:] = raw[half:, :].T

    def emission(scores, at):
        top = jnp.max(jnp.maximum(scores[0], scores[1]), axis=1, keepdims=True)
        here = pl.ds(pl.multiple_of(at, rows), rows)
        em[here, :half] = jnp.exp(scores[0] - top)
        em[here, half:] = jnp.exp(scores[1] - top)

    score_copy.wait_recv()
    line_copy.wait_recv()
    emission(sc, o * rows)
    trans_copy.wait_recv()

    @pl.when(s == 1)
    def _():
        wt[:, :half] = raw[:half, :].T

    flag_pad[...] = jnp.ones_like(flag_pad)
    y[:, :PAD] = jnp.ones((streams, PAD, states), F32)
    y[:, PAD + 2 * frames :] = jnp.ones((streams, PAD, states), F32)

    @pl.when(has_source)
    def _():
        flag_copy.wait_recv()
        for core in range(2):
            pltpu.make_async_copy(sc.at[core], halo.at[core], recv.at[6 + core]).wait()

    @pl.when(jnp.logical_not(has_source))
    def _():
        flag_in[s] = jnp.ones((streams, frames, LANES), F32)
        halo[...] = jnp.zeros_like(halo)

    for h in range(2):
        for b in range(streams):
            flag_pad[b, PAD + h * frames : PAD + (h + 1) * frames] = flag_in[h, b]
    emission(halo, s * rows)

    pieces = [(h, b, (h * streams + b) * frames) for h in range(2) for b in range(streams)]

    def spread(a):
        return jnp.concatenate([a] * (chunk // LANES), axis=1)

    def chain(weights, forward):
        d = -1 if forward else 1
        held = 1 if forward else 0
        if forward:
            prior = lines[...]
            prior = prior / jnp.sum(prior, axis=1, keepdims=True)
        else:
            prior = jnp.full((8, states), 1.0 / states, F32)
        base = prior[0:1]

        for h, b, r in pieces:
            first = PAD + h * frames + (0 if forward else 1)
            mask[r : r + frames] = flag_pad[b, first : first + frames]
            x0 = em[r : r + frames] * base
            xb[0, r : r + frames] = x0.astype(BF16)
            inv[r : r + frames] = jnp.broadcast_to(
                1.0 / jnp.sum(x0, axis=1, keepdims=True), (frames, LANES)
            )

        def step(now, later, last):
            sums = [None] * len(pieces)
            for n in range(0, states, chunk):
                cols = slice(n, n + chunk)
                out = jnp.dot(xb[now], weights[:, cols], preferred_element_type=F32)
                for h, b, r in pieces:
                    at = PAD + h * frames
                    y[b, at : at + frames, cols] = out[r : r + frames] * spread(inv[r : r + frames])
                for k, (h, b, r) in enumerate(pieces):
                    if last and h != held:
                        continue
                    at = PAD + h * frames + d
                    reset = spread(mask[r : r + frames]) > 0.5
                    value = jnp.where(reset, base[:, cols], y[b, at : at + frames, cols])
                    if last and not forward:
                        fin[b * frames : (b + 1) * frames, cols] = value
                        continue
                    value = em[r : r + frames, cols] * value
                    if last:
                        fin[b * frames : (b + 1) * frames, cols] = value
                    else:
                        xb[later, r : r + frames, cols] = value.astype(BF16)
                    part = sum(value[:, i : i + LANES] for i in range(0, chunk, LANES))
                    sums[k] = part if sums[k] is None else sums[k] + part
            for k, (h, b, r) in enumerate(pieces):
                if sums[k] is None:
                    continue
                norm = jnp.sum(sums[k], axis=1, keepdims=True)
                if last:
                    at = b * frames
                    fin[at : at + frames, :states] = fin[at : at + frames, :states] / norm
                    fin[at : at + frames, states:] = jnp.broadcast_to(jnp.log(norm), (frames, LANES))
                else:
                    inv[r : r + frames] = jnp.broadcast_to(1.0 / norm, (frames, LANES))

        def two(i, carry):
            step(0, 1, False)
            step(1, 0, False)
            return carry

        turns = MAXLEN - 2
        lax.fori_loop(0, turns // 2, two, 0)
        if turns % 2:
            step(0, 1, False)
        step(turns % 2, 1 - turns % 2, True)
        if not forward:
            fin[:, states:] = jnp.zeros((rows, LANES), F32)

    @pl.when(s == 0)
    def _():
        chain(raw, True)

    @pl.when(s == 1)
    def _():
        chain(wt, False)

    fin_copy = remote(fin, fin_in, 5, (c, o))
    fin_copy.start()
    fin_copy.wait_recv()
    for b in range(streams):
        at = b * frames
        rows_b = slice(at, at + frames)
        product = fin[rows_b, :states] * fin_in[rows_b, :states]
        scale = 1.0 / jnp.sum(product, axis=1, keepdims=True)
        post[b] = (fin[rows_b, mine] * fin_in[rows_b, mine] * scale).astype(BF16)

    part = frames // 2
    row_e = lax.broadcasted_iota(jnp.int32, (part, LANES), 0)
    col_e = lax.broadcasted_iota(jnp.int32, (part, LANES), 1)
    for b in range(streams):
        at = pl.ds(pl.multiple_of(b * frames + s * part, part), part)
        logs = fin[at, states:] + fin_in[at, states:]
        line = jnp.sum(jnp.where(row_e == col_e, logs, 0.0), axis=0, keepdims=True)
        evid[b : b + 1, :] = line[:, :part]

    for copy in (trans_copy, line_copy, score_copy, fin_copy):
        copy.wait_send()

    @pl.when(has_target)
    def _():
        flag_copy.wait_send()

    @pl.when(has_next)
    def _():
        next_copy.wait_send()

    @pl.when(has_prev)
    def _():
        prev_copy.wait_send()


def per_device(features, gauss_means, precisions, transitions, initial, reset_flags):
    streams, frames, width = features.shape
    half, states = transitions.shape
    rows = streams * frames
    blocks = lax.axis_size("tm")
    vmem = pl.BlockSpec(memory_space=pltpu.VMEM)
    return pl.pallas_call(
        functools.partial(kernel, blocks),
        out_shape=(
            jax.ShapeDtypeStruct((streams, frames, half), BF16),
            jax.ShapeDtypeStruct((streams, frames // 2), F32),
        ),
        in_specs=[pl.BlockSpec(memory_space=pltpu.HBM)] * 6,
        out_specs=(vmem, vmem),
        scratch_shapes=[
            pltpu.VMEM((half, width), F32),
            pltpu.VMEM((half, width), F32),
            pltpu.VMEM((half,), BF16),
            pltpu.VMEM((streams, frames), jnp.int32),
            pltpu.VMEM((streams, frames, width), F32),
            pltpu.VMEM((2, streams, frames, LANES), F32),
            pltpu.VMEM((states, states), BF16),
            pltpu.VMEM((states, states), BF16),
            pltpu.VMEM((8, states), F32),
            pltpu.VMEM((half, 2 * width), BF16),
            pltpu.VMEM((half, 2 * width), BF16),
            pltpu.VMEM((2, rows, half), F32),
            pltpu.VMEM((2, rows, half), F32),
            pltpu.VMEM((2 * rows, states), F32),
            pltpu.VMEM((2, 2 * rows, states), BF16),
            pltpu.VMEM((streams, 2 * frames + 2 * PAD, states), F32),
            pltpu.VMEM((2 * rows, LANES), F32),
            pltpu.VMEM((streams, 2 * frames + 2 * PAD, LANES), F32),
            pltpu.VMEM((2 * rows, LANES), F32),
            pltpu.VMEM((rows, states + LANES), F32),
            pltpu.VMEM((rows, states + LANES), F32),
            pltpu.SemaphoreType.DMA((8,)),
            pltpu.SemaphoreType.DMA((8,)),
            pltpu.SemaphoreType.DMA((6,)),
        ],
        compiler_params=pltpu.CompilerParams(
            collective_id=0, has_side_effects=True, vmem_limit_bytes=63 * 1024 * 1024
        ),
    )(features, gauss_means, precisions, transitions, initial, reset_flags)


def solution(mesh):
    return jax.shard_map(
        per_device,
        mesh=mesh,
        in_specs=(
            P(None, "tm", None),
            P("state", None),
            P("state", None),
            P("state", None),
            P("state"),
            P(None, "tm"),
        ),
        out_specs=(P(None, "tm", "state"), P(None, ("tm", "state"))),
        check_vma=False,
    )
```

```python
import functools

import jax
import jax.numpy as jnp
from jax import lax
from jax.experimental import pallas as pl
from jax.experimental.pallas import tpu as pltpu
from jax.sharding import PartitionSpec as P

MAXLEN = 16
ACOUSTIC = 0.1
MESH = pl.DeviceIdType.MESH
F32 = jnp.float32
BF16 = jnp.bfloat16
PAD = 8
LANES = 128


def split(a):
    hi = a.astype(BF16)
    return hi, (a - hi.astype(F32)).astype(BF16)


def dot_t(a, b):
    return lax.dot_general(a, b, (((1,), (1,)), ((), ())), preferred_element_type=F32)


def kernel(
    blocks, feat, means_hbm, prec_hbm, trans, init_hbm, flags_hbm, post, evid,
    means, prec, init, flags, xin, flag_in, raw, wt, lines, w_hi, w_lo, sc, sent, halo, em, xb, y, inv, flag_pad, mask, fin, fin_in,
    send, recv, load,
):
    c = lax.axis_index("tm")
    s = lax.axis_index("state")
    o = 1 - s
    target = c + 1 - 2 * s
    source = c - 1 + 2 * s
    has_target = jnp.logical_and(target >= 0, target < blocks)
    has_source = jnp.logical_and(source >= 0, source < blocks)

    streams, frames, width = feat.shape
    half = trans.shape[0]
    states = trans.shape[1]
    rows = streams * frames
    chunk = min(256, states)

    barrier = pltpu.get_barrier_semaphore()

    @pl.when(has_source)
    def _():
        pl.semaphore_signal(barrier, inc=1, device_id=(source, s), device_id_type=MESH)

    pl.semaphore_signal(barrier, inc=1, device_id=(c, o), device_id_type=MESH)

    mine = pl.ds(pl.multiple_of(s * half, half), half)
    theirs = pl.ds(pl.multiple_of(o * half, half), half)

    loads = [
        pltpu.make_async_copy(src, dst, load.at[k])
        for k, (src, dst) in enumerate(
            (
                (flags_hbm, flags),
                (init_hbm, init),
                (prec_hbm, prec),
                (means_hbm, means),
                (trans, raw.at[mine]),
                (feat, xin),
            )
        )
    ]
    for copy in loads:
        copy.start()

    row_t = lax.broadcasted_iota(jnp.int32, (frames, frames), 0)
    col_t = lax.broadcasted_iota(jnp.int32, (frames, frames), 1)
    loads[0].wait()
    for b in range(streams):
        line = jnp.broadcast_to(flags[b : b + 1, :].astype(F32), (frames, frames))
        column = jnp.sum(jnp.where(row_t == col_t, line, 0.0), axis=1, keepdims=True)
        flag_in[o, b] = jnp.broadcast_to(column, (frames, LANES))
    loads[1].wait()
    lines[:, mine] = jnp.broadcast_to(init[...].astype(F32).reshape(1, half), (8, half))

    def remote(src, dst, k, who):
        return pltpu.make_async_remote_copy(
            src_ref=src, dst_ref=dst, send_sem=send.at[k], recv_sem=recv.at[k],
            device_id=who, device_id_type=MESH,
        )

    halo_copy = remote(sent, halo, 0, (target, s))
    trans_copy = remote(trans, raw.at[mine], 2, (c, o))
    line_copy = remote(lines.at[:, mine], lines.at[:, mine], 3, (c, o))
    score_copy = remote(sc.at[s], sc.at[s], 4, (c, o))
    loads[2].wait()
    loads[3].wait()
    p = prec[...]
    m = means[...]
    pm = p * m
    hi, lo = split(-0.5 * p)
    w_hi[:, :width] = hi
    w_lo[:, :width] = lo
    hi, lo = split(pm)
    w_hi[:, width:] = hi
    w_lo[:, width:] = lo
    offset = 0.5 * jnp.sum(jnp.log(p) - pm * m, axis=1, keepdims=True)
    offset = jnp.broadcast_to(offset, (half, LANES)).T[0:1]
    loads[5].wait()
    x = xin[...].reshape(rows, width)
    sq_hi, sq_lo = split(x * x)
    x_hi, x_lo = split(x)
    left_hi = jnp.concatenate([sq_hi, x_hi], axis=1)
    left_lo = jnp.concatenate([sq_lo, x_lo], axis=1)
    both = dot_t(jnp.concatenate([left_hi, left_lo], axis=0), w_hi[...])
    total = both[:rows] + (both[rows:] + dot_t(left_hi, w_lo[...]))
    sc[s] = ACOUSTIC * (total + offset)

    pl.semaphore_wait(barrier, 1 + has_target.astype(jnp.int32))
    score_copy.start()
    line_copy.start()
    for b in range(streams):
        sent[b * frames : (b + 1) * frames, states:] = flag_in[o, b].astype(BF16)
    score_copy.wait_recv()
    top = jnp.max(jnp.maximum(sc[0], sc[1]), axis=1, keepdims=True)
    here = pl.ds(pl.multiple_of(o * rows, rows), rows)
    for core in range(2):
        cols = slice(core * half, (core + 1) * half)
        value = jnp.exp(sc[core] - top)
        em[here, cols] = value
        sent[:, cols] = value.astype(BF16)

    @pl.when(has_target)
    def _():
        halo_copy.start()

    trans_copy.start()
    loads[4].wait()

    @pl.when(s == 1)
    def _():
        wt[:, half:] = raw[half:, :].T

    line_copy.wait_recv()
    trans_copy.wait_recv()

    @pl.when(s == 1)
    def _():
        wt[:, :half] = raw[:half, :].T

    flag_pad[...] = jnp.ones_like(flag_pad)
    y[:, :PAD] = jnp.ones((streams, PAD, states), F32)
    y[:, PAD + 2 * frames :] = jnp.ones((streams, PAD, states), F32)

    @pl.when(has_source)
    def _():
        halo_copy.wait_recv()

    @pl.when(jnp.logical_not(has_source))
    def _():
        halo[...] = jnp.ones_like(halo)

    for b in range(streams):
        flag_in[s, b] = halo[b * frames : (b + 1) * frames, states:].astype(F32)
    for h in range(2):
        for b in range(streams):
            flag_pad[b, PAD + h * frames : PAD + (h + 1) * frames] = flag_in[h, b]
    em[pl.ds(pl.multiple_of(s * rows, rows), rows)] = halo[:, :states].astype(F32)

    pieces = [(h, b, (h * streams + b) * frames) for h in range(2) for b in range(streams)]

    def spread(a):
        return jnp.concatenate([a] * (chunk // LANES), axis=1)

    def chain(weights, forward):
        d = -1 if forward else 1
        held = 1 if forward else 0
        if forward:
            prior = lines[...]
            prior = prior / jnp.sum(prior, axis=1, keepdims=True)
        else:
            prior = jnp.full((8, states), 1.0 / states, F32)
        base = prior[0:1]

        for h, b, r in pieces:
            first = PAD + h * frames + (0 if forward else 1)
            mask[r : r + frames] = flag_pad[b, first : first + frames]
            x0 = em[r : r + frames] * base
            xb[0, r : r + frames] = x0.astype(BF16)
            inv[r : r + frames] = jnp.broadcast_to(
                1.0 / jnp.sum(x0, axis=1, keepdims=True), (frames, LANES)
            )

        def step(now, later, last):
            sums = [None] * len(pieces)
            for n in range(0, states, chunk):
                cols = slice(n, n + chunk)
                out = jnp.dot(xb[now], weights[:, cols], preferred_element_type=F32)
                for h, b, r in pieces:
                    at = PAD + h * frames
                    y[b, at : at + frames, cols] = out[r : r + frames] * spread(inv[r : r + frames])
                for k, (h, b, r) in enumerate(pieces):
                    if last and h != held:
                        continue
                    at = PAD + h * frames + d
                    reset = spread(mask[r : r + frames]) > 0.5
                    value = jnp.where(reset, base[:, cols], y[b, at : at + frames, cols])
                    if last and not forward:
                        fin[b * frames : (b + 1) * frames, cols] = value
                        continue
                    value = em[r : r + frames, cols] * value
                    if last:
                        fin[b * frames : (b + 1) * frames, cols] = value
                    else:
                        xb[later, r : r + frames, cols] = value.astype(BF16)
                    part = sum(value[:, i : i + LANES] for i in range(0, chunk, LANES))
                    sums[k] = part if sums[k] is None else sums[k] + part
            for k, (h, b, r) in enumerate(pieces):
                if sums[k] is None:
                    continue
                norm = jnp.sum(sums[k], axis=1, keepdims=True)
                if last:
                    at = b * frames
                    fin[at : at + frames, :states] = fin[at : at + frames, :states] / norm
                    fin[at : at + frames, states:] = jnp.broadcast_to(jnp.log(norm), (frames, LANES))
                else:
                    inv[r : r + frames] = jnp.broadcast_to(1.0 / norm, (frames, LANES))

        def two(i, carry):
            step(0, 1, False)
            step(1, 0, False)
            return carry

        turns = MAXLEN - 2
        lax.fori_loop(0, turns // 2, two, 0)
        if turns % 2:
            step(0, 1, False)
        step(turns % 2, 1 - turns % 2, True)
        if not forward:
            fin[:, states:] = jnp.zeros((rows, LANES), F32)

    @pl.when(s == 0)
    def _():
        chain(raw, True)

    @pl.when(s == 1)
    def _():
        chain(wt, False)

    fin_copy = remote(fin, fin_in, 5, (c, o))
    fin_copy.start()
    fin_copy.wait_recv()
    for b in range(streams):
        at = b * frames
        rows_b = slice(at, at + frames)
        product = fin[rows_b, :states] * fin_in[rows_b, :states]
        scale = 1.0 / jnp.sum(product, axis=1, keepdims=True)
        post[b] = (fin[rows_b, mine] * fin_in[rows_b, mine] * scale).astype(BF16)

    part = frames // 2
    row_e = lax.broadcasted_iota(jnp.int32, (part, LANES), 0)
    col_e = lax.broadcasted_iota(jnp.int32, (part, LANES), 1)
    for b in range(streams):
        at = pl.ds(pl.multiple_of(b * frames + s * part, part), part)
        logs = fin[at, states:] + fin_in[at, states:]
        line = jnp.sum(jnp.where(row_e == col_e, logs, 0.0), axis=0, keepdims=True)
        evid[b : b + 1, :] = line[:, :part]

    for copy in (trans_copy, line_copy, score_copy, fin_copy):
        copy.wait_send()

    @pl.when(has_target)
    def _():
        halo_copy.wait_send()


def per_device(features, gauss_means, precisions, transitions, initial, reset_flags):
    streams, frames, width = features.shape
    half, states = transitions.shape
    rows = streams * frames
    blocks = lax.axis_size("tm")
    vmem = pl.BlockSpec(memory_space=pltpu.VMEM)
    return pl.pallas_call(
        functools.partial(kernel, blocks),
        out_shape=(
            jax.ShapeDtypeStruct((streams, frames, half), BF16),
            jax.ShapeDtypeStruct((streams, frames // 2), F32),
        ),
        in_specs=[pl.BlockSpec(memory_space=pltpu.HBM)] * 6,
        out_specs=(vmem, vmem),
        scratch_shapes=[
            pltpu.VMEM((half, width), F32),
            pltpu.VMEM((half, width), F32),
            pltpu.VMEM((half,), BF16),
            pltpu.VMEM((streams, frames), jnp.int32),
            pltpu.VMEM((streams, frames, width), F32),
            pltpu.VMEM((2, streams, frames, LANES), F32),
            pltpu.VMEM((states, states), BF16),
            pltpu.VMEM((states, states), BF16),
            pltpu.VMEM((8, states), F32),
            pltpu.VMEM((half, 2 * width), BF16),
            pltpu.VMEM((half, 2 * width), BF16),
            pltpu.VMEM((2, rows, half), F32),
            pltpu.VMEM((rows, states + LANES), BF16),
            pltpu.VMEM((rows, states + LANES), BF16),
            pltpu.VMEM((2 * rows, states), F32),
            pltpu.VMEM((2, 2 * rows, states), BF16),
            pltpu.VMEM((streams, 2 * frames + 2 * PAD, states), F32),
            pltpu.VMEM((2 * rows, LANES), F32),
            pltpu.VMEM((streams, 2 * frames + 2 * PAD, LANES), F32),
            pltpu.VMEM((2 * rows, LANES), F32),
            pltpu.VMEM((rows, states + LANES), F32),
            pltpu.VMEM((rows, states + LANES), F32),
            pltpu.SemaphoreType.DMA((6,)),
            pltpu.SemaphoreType.DMA((6,)),
            pltpu.SemaphoreType.DMA((6,)),
        ],
        compiler_params=pltpu.CompilerParams(
            collective_id=0, has_side_effects=True, vmem_limit_bytes=63 * 1024 * 1024
        ),
    )(features, gauss_means, precisions, transitions, initial, reset_flags)


def solution(mesh):
    return jax.shard_map(
        per_device,
        mesh=mesh,
        in_specs=(
            P(None, "tm", None),
            P("state", None),
            P("state", None),
            P("state", None),
            P("state"),
            P(None, "tm"),
        ),
        out_specs=(P(None, "tm", "state"), P(None, ("tm", "state"))),
        check_vma=False,
    )
```
